768 devices in a mesh: rep: 192 (over x_hi, z, y), fsdp: 4 (over x_lo, core).
Axes of the slice: x: 4 (x_hi: 2, x_lo: 2; x = x_hi * 2 + x_lo), y: 8, z: 12, core: 2. Of those that a mesh axis runs over, the one named last changes fastest.
Arguments:
- gradient: bfloat16 [192, 4, 128, 5120], P('rep', 'fsdp'), may hold values from -6 to 6
- momentum: float32 [192, 128, 5120], P('rep', None, 'fsdp'), may hold values from -6 to 6
- params: float32 [128, 5120], P(None, 'fsdp'), may hold values from -6 to 6
Outputs:
- new_params: float32 [128, 5120], P(None, 'fsdp')
- new_momentum: float32 [192, 128, 5120], P('rep', None, 'fsdp')
The draws below stay inside these ranges and needn't reach their ends.
All inputs are finite; a program needn't handle non-finite values.
Results may differ from the reference program's by a relative error of at most 0.0003.
Values sent between devices are 32-bit elements; how exact they have to be, the bound alone decides.
A program may use at most 64 MiB of HBM per device.

```python
import jax
import jax.numpy as jnp
from jax import lax

COLS = 5120
TILE = 128
KEEP = 32
ROWS = 128
N_REP = 192
N_FSDP = 4


def level_of(rng, extent, cuts, low, largest):
    loudness, own = 1.0, jax.random.fold_in(rng, 6)
    for position, shards_of in cuts:
        draws = jnp.exp(jax.random.uniform(jax.random.fold_in(own, position), (shards_of,), jnp.float32, low / len(cuts), largest / len(cuts)))
        loudness = loudness * jnp.repeat(draws, extent[position] // shards_of).reshape([-1 if axis == position else 1 for axis in range(len(extent))])
    return loudness


def bell_draw(stream_key, dims, spread, reach, split=(), held_as=jnp.bfloat16):
    loudness = level_of(stream_key, dims, split, -0.22, 0.18) if split else 1.0
    entries = jax.random.normal(stream_key, dims, jnp.float32) * spread * loudness
    return jnp.minimum(jnp.maximum(entries, -reach), reach).astype(held_as)


def setup_inputs(seed: int = 0) -> dict:
    key_of = jax.random.split(jax.random.key(seed), 4)
    return {
        "gradient": bell_draw(key_of[0], (N_REP, N_FSDP, ROWS, COLS), 1.0, 6.0, ((0, 192), (1, 4))),
        "momentum": bell_draw(key_of[1], (N_REP, ROWS, COLS), 1.0, 6.0, ((0, 192), (2, 4)), jnp.float32),
        "params": bell_draw(key_of[2], (ROWS, COLS), 1.0, 6.0, ((1, 4),), jnp.float32),
    }


def make_basis():
    k = jnp.arange(KEEP, dtype=jnp.float32)[:, None]
    n = jnp.arange(TILE, dtype=jnp.float32)[None, :]
    table = jnp.cos(jnp.pi * (2.0 * n + 1.0) * k / (2.0 * TILE)) * jnp.sqrt(2.0 / TILE)
    return table * jnp.where(k == 0, jnp.sqrt(0.5), 1.0)

def encode(matrix, basis):
    tiles = matrix.reshape(matrix.shape[0] // TILE, TILE, matrix.shape[1] // TILE, TILE)
    return jnp.einsum('kr,arbc,lc->abkl', basis, tiles, basis, precision=lax.Precision.HIGHEST)

def decode(coefs, basis):
    tiles = jnp.einsum('kr,abkl,lc->arbc', basis, coefs, basis, precision=lax.Precision.HIGHEST)
    return tiles.reshape(tiles.shape[0] * TILE, tiles.shape[2] * TILE)

def reference(gradient, momentum, params):
    basis = make_basis()

    def one_replica(pair):
        grads, moment_old = pair
        moment = 0.9 * moment_old + lax.optimization_barrier(jnp.sum(grads.astype(jnp.float32), axis=0))
        coefs = encode(moment, basis)
        return (moment - decode(coefs, basis), coefs)
    new_momentum, coefs = lax.map(one_replica, (gradient, momentum))
    total = lax.optimization_barrier(jnp.sum(coefs, axis=0))
    new_params = params - 1.0 / jnp.sqrt(jnp.float32(N_REP)) * decode(total, basis)
    return (new_params, new_momentum)
```

```python
import jax
import jax.numpy as jnp
import numpy as np
from jax import lax
from jax.experimental import pallas as pl
from jax.experimental.pallas import tpu as pltpu
from jax.sharding import PartitionSpec as P

MESH = pl.DeviceIdType.MESH
F32, BF16 = jnp.float32, jnp.bfloat16
TILE, KEEP = 128, 32
NXH, NZ, NY = 2, 12, 8
ROWS_XY = [(0, 3), (0, 4), (0, 5), (0, 6), (1, 2), (1, 3), (1, 4), (1, 5), (1, 6), (1, 7)]
NT = 10


def split_np(a):
    a = np.asarray(a, np.float32)
    high = a.astype(jnp.bfloat16)
    low = (a - high.astype(np.float32)).astype(jnp.bfloat16)
    return high, low


def constants():
    k, n = np.arange(KEEP)[:, None], np.arange(TILE)[None, :]
    basis = np.cos(np.pi * (2 * n + 1) * k / (2 * TILE)) * np.sqrt(2 / TILE)
    basis = basis * np.where(k == 0, np.sqrt(0.5), 1.0)
    b1, b2 = split_np(basis)
    zero = np.zeros_like(b1)

    def four(b):
        out = np.zeros((4 * b.shape[0], 4 * b.shape[1]), b.dtype)
        for i in range(4):
            out[i * b.shape[0] : (i + 1) * b.shape[0], i * b.shape[1] : (i + 1) * b.shape[1]] = b
        return out

    right = np.concatenate([four(b1.T), four(b2.T)], 1)
    left = np.block([[b1, b1], [b2, zero]])
    p1, p2 = split_np(basis.T @ basis)
    p_left = np.concatenate([p1, p1, p2], 1)
    p_right = np.concatenate([p1, p1, p2], 0)
    d_left = np.concatenate([b1.T, b1.T, b2.T], 1)
    d_right = np.concatenate([four(b1), four(b1), four(b2)], 0)
    return right, left, p_left, p_right, d_left, d_right


def split(x):
    high = x.astype(BF16)
    return high, (x - high.astype(F32)).astype(BF16)


def dot(a, b):
    return jnp.dot(a, b, preferred_element_type=F32)


def columns_of(g, right, low):
    parts = []
    for q in range(3):
        width = 512 if q < 2 else 256
        x = g[:, 512 * q : 512 * q + width]
        if low:
            y = dot(x, right[:width, :])
            parts.append(y[:, :128] + y[:, 128:])
        else:
            parts.append(dot(x, right[:width, :128]))
    return jnp.concatenate(parts, 1)


def rows_of(y, left):
    y1, y2 = split(y)
    z = dot(left, jnp.concatenate([y1, y2], 0))
    return z[:KEEP] + z[KEEP:]


def chunks_of(z):
    tail = z[:, 256:384]
    tail = tail[:16] + pltpu.roll(tail[16:], 64, 1)
    return (
        z[:, :128].reshape(4, 8, 128),
        z[:, 128:256].reshape(4, 8, 128),
        tail.reshape(2, 8, 128),
    )


def kernel(
    scale, g_hbm, m_hbm, w_hbm, c_right, c_left, c_pl, c_pr, c_dl, c_dr,
    new_w, new_m,
    gs, ms, ws, right, left, p_left, p_right, d_left, d_right,
    cf, rc, sa, ra, sb, rb, sc, rt,
    gst, rg, xs, xt, om, ow,
    load_sem, core_s, core_r, a_sem, b_sem, c_sem, x_s, x_r, out_sem,
):
    rep, f = lax.axis_index("rep"), lax.axis_index("fsdp")
    xh, z, y = rep // (NZ * NY), (rep // NY) % NZ, rep % NY
    xl, c = f // 2, f % 2

    def device(dxh, dz, dy, dxl, dc):
        return ((dxh * NZ + dz) * NY + dy, dxl * 2 + dc)

    sibling = device(xh, z, y, xl, 1 - c)
    across = device(xh, z, y, 1 - xl, c)
    owner = jnp.logical_or(
        jnp.logical_and(xh == 0, jnp.logical_and(y >= 3, y <= 6)),
        jnp.logical_and(xh == 1, y >= 2),
    )
    mine = jnp.where(owner, jnp.where(xh == 0, y - 3, y + 2), 0)
    chip = (xh * NY + y) * 2 + xl

    blocks = [f, (1 - xl) * 2 + c, xl * 2 + 1 - c, (1 - xl) * 2 + 1 - c]
    loads = [
        pltpu.make_async_copy(
            g_hbm.at[0, 0, :, pl.ds(pl.multiple_of(b * 1280, 1280), 1280)], gs.at[i], load_sem.at[i]
        )
        for i, b in enumerate(blocks)
    ]
    consts = [
        pltpu.make_async_copy(src, dst, load_sem.at[4 + i])
        for i, (src, dst) in enumerate(
            [(c_right, right), (c_left, left), (m_hbm.at[0], ms), (c_pl, p_left), (c_pr, p_right),
             (c_dl, d_left), (c_dr, d_right), (w_hbm, ws)]
        )
    ]
    for copy in consts[:1] + loads + consts[1:]:
        copy.start()

    barrier = pltpu.get_barrier_semaphore()

    def greet(to):
        pl.semaphore_signal(barrier, inc=1, device_id=to, device_id_type=MESH)

    greet(sibling)
    for dx in range(2):
        for dy in range(NY):
            for dl in range(2):
                if dx or dy or dl:
                    greet(device((xh + dx) % 2, z, (y + dy) % NY, (xl + dl) % 2, c))

    @pl.when(owner)
    def _():
        for dz in range(1, NZ):
            greet(device(xh, (z + dz) % NZ, y, xl, c))

    consts[0].wait()
    ys = []
    for i in (2, 3):
        loads[i].wait()
        ys.append(columns_of(gs[i], right, True))
    consts[1].wait()
    zs = rows_of(jnp.concatenate(ys, 1), left[...])
    for i in (2, 3):
        q = chunks_of(zs[:, 384 * (i - 2) : 384 * (i - 1)])
        cf[i, 0:4], cf[i, 4:8], cf[i, 8:10] = q

    @pl.when(owner)
    def _():
        pl.semaphore_wait(barrier, 32 + NZ - 1)

    @pl.when(jnp.logical_not(owner))
    def _():
        pl.semaphore_wait(barrier, 32)

    def send(src, dst, s, r, to):
        return pltpu.make_async_remote_copy(
            src_ref=src, dst_ref=dst, send_sem=s, recv_sem=r, device_id=to, device_id_type=MESH
        )

    core0 = send(cf.at[pl.ds(2, 2)], rc, core_s.at[0], core_r.at[0], sibling)
    core0.start()
    for t in range(NT):
        gst[0, t] = gs[3, :, 128 * t : 128 * t + 128].astype(F32)
    core1 = send(gst.at[0], rg.at[0], core_s.at[1], core_r.at[1], sibling)
    core1.start()
    ys = []
    for i in (0, 1):
        loads[i].wait()
        ys.append(columns_of(gs[i], right, True))
    consts[2].wait()
    m1, m2 = split(0.9 * ms[...])
    ys[0] = ys[0] + columns_of(m1, right, True) + columns_of(m2, right, False)
    zs = rows_of(jnp.concatenate(ys, 1), left[...])
    core0.wait_recv()
    for i in (0, 1):
        q = chunks_of(zs[:, 384 * i : 384 * (i + 1)])
        sa[i, 0:4] = q[0] + rc[i, 0:4]
        sa[i, 4:8] = q[1] + rc[i, 4:8]
        sa[i, 8:10] = q[2] + rc[i, 8:10]

    for i in range(2):
        for j, (ox, oy) in enumerate(ROWS_XY):
            to = device(ox, z, oy, xl if i == 0 else 1 - xl, c)
            copy = send(sa.at[i, j], ra.at[chip], a_sem.at[i], a_sem.at[2], to)
            if i == 0:
                here = jnp.logical_and(xh == ox, y == oy)

                @pl.when(jnp.logical_not(here))
                def _():
                    copy.start()

                @pl.when(here)
                def _():
                    ra[chip] = sa[0, j]
            else:
                copy.start()

    for t in range(NT):
        gst[1, t] = gs[2, :, 128 * t : 128 * t + 128].astype(F32)
    core2 = send(gst.at[1], rg.at[1], core_s.at[2], core_r.at[2], sibling)
    core2.start()
    core1.wait_recv()
    swaps = []
    for t in range(NT):
        xs[t] = gs[1, :, 128 * t : 128 * t + 128].astype(F32) + rg[0, t]
        swaps.append(send(xs.at[t], xt.at[t], x_s.at[t], x_r.at[t], across))
        swaps[-1].start()

    @pl.when(owner)
    def _():
        send(ra.at[pl.ds(0, 31)], ra.at[pl.ds(0, 31)], a_sem.at[0], a_sem.at[2], sibling).wait_recv()
        total = ra[0]
        for i in range(1, 32):
            total = total + ra[i]
        sb[...] = total
        rb[z] = total
        for dz in list(range(1, 7)) + list(range(11, 6, -1)):
            send(sb, rb.at[z], b_sem.at[0], b_sem.at[1], device(xh, (z + dz) % NZ, y, xl, c)).start()
        send(rb.at[pl.ds(0, 11)], rb.at[pl.ds(0, 11)], b_sem.at[0], b_sem.at[1], sibling).wait_recv()
        total = rb[0]
        for i in range(1, NZ):
            total = total + rb[i]
        sc[...] = total
        rt[mine] = total
        for dx in range(2):
            for dy in range(NY):
                if dx or dy:
                    to = device((xh + dx) % 2, z, (y + dy) % NY, xl, c)
                    send(sc, rt.at[mine], c_sem.at[0], c_sem.at[1], to).start()

    core2.wait_recv()
    consts[3].wait()
    consts[4].wait()
    outs = []
    for t in range(NT):
        cols = pl.ds(128 * t, 128)
        swaps[t].wait_recv()
        x = 0.9 * ms[:, cols] + ((gs[0, :, cols].astype(F32) + rg[1, t]) + xt[t])
        x1, x2 = split(x)
        u1, u2 = split(dot(p_left[...], jnp.concatenate([x1, x2, x1], 0)))
        om[:, cols] = x - dot(jnp.concatenate([u1, u2, u1], 1), p_right[...])
        outs.append(pltpu.make_async_copy(om.at[:, cols], new_m.at[0, :, cols], out_sem.at[t]))
        outs[-1].start()

    for i in range(5, 8):
        consts[i].wait()

    @pl.when(owner)
    def _():
        send(rt.at[pl.ds(0, 9)], rt.at[pl.ds(0, 9)], c_sem.at[0], c_sem.at[1], sibling).wait_recv()

    @pl.when(jnp.logical_not(owner))
    def _():
        send(rt, rt, c_sem.at[0], c_sem.at[1], sibling).wait_recv()

    tail = rt[8:10].reshape(16, 128)
    zt = jnp.concatenate(
        [rt[0:4].reshape(32, 128), rt[4:8].reshape(32, 128), jnp.concatenate([tail, pltpu.roll(tail, 64, 1)], 0)], 1
    )
    z1, z2 = split(zt)
    v1, v2 = split(dot(d_left[...], jnp.concatenate([z1, z2, z1], 0)))
    for q in range(3):
        width = 512 if q < 2 else 256
        part = slice(128 * q, 128 * q + 128)
        low = dot(jnp.concatenate([v1[:, part], v2[:, part], v1[:, part]], 1), d_right[:, :width])
        cols = pl.ds(512 * q, width)
        ow[:, cols] = ws[:, cols] - scale * low
        outs.append(pltpu.make_async_copy(ow.at[:, cols], new_w.at[:, cols], out_sem.at[NT + q]))
        outs[-1].start()

    for copy in (core0, core1, core2, *swaps):
        copy.wait_send()
    send(sa.at[1], sa.at[1], a_sem.at[1], a_sem.at[2], sibling).wait_send()

    @pl.when(owner)
    def _():
        send(sa.at[0, pl.ds(0, 9)], sa.at[0, pl.ds(0, 9)], a_sem.at[0], a_sem.at[2], sibling).wait_send()
        send(rb.at[pl.ds(0, 11)], rb.at[pl.ds(0, 11)], b_sem.at[0], b_sem.at[1], sibling).wait_send()
        send(ra.at[pl.ds(0, 15)], ra.at[pl.ds(0, 15)], c_sem.at[0], c_sem.at[1], sibling).wait_send()

    @pl.when(jnp.logical_not(owner))
    def _():
        send(sa.at[0], sa.at[0], a_sem.at[0], a_sem.at[2], sibling).wait_send()

    for copy in outs:
        copy.wait()


def solution(mesh):
    scale = float(1.0 / np.sqrt(np.float32(mesh.shape["rep"])))
    consts = constants()

    def per_device(gradient, momentum, params):
        vmem, dma = pltpu.VMEM, pltpu.SemaphoreType.DMA
        tiles = (NT, TILE, TILE)
        chunk = (8, 128)
        slab = (TILE, NT * TILE)

        def body(*refs):
            kernel(scale, *refs)

        new_w, new_m = pl.pallas_call(
            body,
            out_shape=(
                jax.ShapeDtypeStruct(params.shape, F32),
                jax.ShapeDtypeStruct(momentum.shape, F32),
            ),
            in_specs=[pl.BlockSpec(memory_space=pl.ANY)] * 9,
            out_specs=(pl.BlockSpec(memory_space=pl.ANY),) * 2,
            scratch_shapes=[
                vmem((4, *slab), BF16), vmem(slab, F32), vmem(slab, F32),
                *[vmem(a.shape, BF16) for a in consts],
                vmem((4, NT, *chunk), F32),
                vmem((2, NT, *chunk), F32),
                vmem((2, NT, *chunk), F32),
                vmem((32, *chunk), F32),
                vmem(chunk, F32),
                vmem((NZ, *chunk), F32),
                vmem(chunk, F32),
                vmem((NT, *chunk), F32),
                vmem((2, *tiles), F32),
                vmem((2, *tiles), F32),
                vmem(tiles, F32),
                vmem(tiles, F32),
                vmem(slab, F32),
                vmem(slab, F32),
                dma((12,)), dma((3,)), dma((3,)), dma((3,)), dma((2,)), dma((2,)),
                dma((NT,)), dma((NT,)), dma((NT + 3,)),
            ],
            compiler_params=pltpu.CompilerParams(
                collective_id=0, has_side_effects=True, vmem_limit_bytes=40 * 2**20
            ),
        )(gradient, momentum, params, *[jnp.asarray(a) for a in consts])
        return new_w, new_m

    return jax.shard_map(
        per_device,
        mesh=mesh,
        in_specs=(P("rep", "fsdp", None, None), P("rep", None, "fsdp"), P(None, "fsdp")),
        out_specs=(P(None, "fsdp"), P("rep", None, "fsdp")),
        check_vma=False,
    )
```

```python
import jax
import jax.numpy as jnp
import numpy as np
from jax import lax
from jax.experimental import pallas as pl
from jax.experimental.pallas import tpu as pltpu
from jax.sharding import PartitionSpec as P

MESH = pl.DeviceIdType.MESH
F32, BF16 = jnp.float32, jnp.bfloat16
TILE, KEEP = 128, 32
NXH, NZ, NY = 2, 12, 8
FIRST, LINES = 7, 5
ROWS_XY = [(i, (FIRST + j) % NY) for i in range(NXH) for j in range(LINES)]
NT = 10


def split_np(a):
    a = np.asarray(a, np.float32)
    high = a.astype(jnp.bfloat16)
    low = (a - high.astype(np.float32)).astype(jnp.bfloat16)
    return high, low


def constants():
    k, n = np.arange(KEEP)[:, None], np.arange(TILE)[None, :]
    basis = np.cos(np.pi * (2 * n + 1) * k / (2 * TILE)) * np.sqrt(2 / TILE)
    basis = basis * np.where(k == 0, np.sqrt(0.5), 1.0)
    b1, b2 = split_np(basis)
    zero = np.zeros_like(b1)

    def four(b):
        out = np.zeros((4 * b.shape[0], 4 * b.shape[1]), b.dtype)
        for i in range(4):
            out[i * b.shape[0] : (i + 1) * b.shape[0], i * b.shape[1] : (i + 1) * b.shape[1]] = b
        return out

    right = np.concatenate([four(b1.T), four(b2.T)], 1)
    left = np.block([[b1, b1], [b2, zero]])
    p1, p2 = split_np(basis.T @ basis)
    p_left = np.concatenate([p1, p1, p2], 1)
    p_right = np.concatenate([p1, p1, p2], 0)
    d_left = np.concatenate([b1.T, b1.T, b2.T], 1)
    d_right = np.concatenate([four(b1), four(b1), four(b2)], 0)
    return right, left, p_left, p_right, d_left, d_right


def split(x):
    high = x.astype(BF16)
    return high, (x - high.astype(F32)).astype(BF16)


def dot(a, b):
    return jnp.dot(a, b, preferred_element_type=F32)


def columns_of(g, right, low):
    parts = []
    for q in range(3):
        width = 512 if q < 2 else 256
        x = g[:, 512 * q : 512 * q + width]
        if low:
            y = dot(x, right[:width, :])
            parts.append(y[:, :128] + y[:, 128:])
        else:
            parts.append(dot(x, right[:width, :128]))
    return jnp.concatenate(parts, 1)


def rows_of(y, left):
    y1, y2 = split(y)
    z = dot(left, jnp.concatenate([y1, y2], 0))
    return z[:KEEP] + z[KEEP:]


def chunks_of(z):
    tail = z[:, 256:384]
    tail = tail[:16] + pltpu.roll(tail[16:], 64, 1)
    return (
        z[:, :128].reshape(4, 8, 128),
        z[:, 128:256].reshape(4, 8, 128),
        tail.reshape(2, 8, 128),
    )


def kernel(
    g_hbm, m_hbm, c_right, c_left, c_pl, c_pr,
    totals, new_m,
    gs, ms, right, left, p_left, p_right,
    cf, rc, sa, ra, sb, rb, sc, rt,
    gst, rg, xs, xt, om,
    load_sem, core_s, core_r, a_sem, b_sem, c_sem, x_s, x_r, out_sem, in_sem,
):
    rep, f = lax.axis_index("rep"), lax.axis_index("fsdp")
    xh, z, y = rep // (NZ * NY), (rep // NY) % NZ, rep % NY
    xl, c = f // 2, f % 2

    def device(dxh, dz, dy, dxl, dc):
        return ((dxh * NZ + dz) * NY + dy, dxl * 2 + dc)

    sibling = device(xh, z, y, xl, 1 - c)
    across = device(xh, z, y, 1 - xl, c)
    line = (y - FIRST + NY) % NY
    owner = line < LINES
    mine = jnp.where(owner, xh * LINES + line, 0)
    chip = (xh * NY + y) * 2 + xl

    blocks = [f, (1 - xl) * 2 + c, xl * 2 + 1 - c, (1 - xl) * 2 + 1 - c]
    loads = [
        pltpu.make_async_copy(
            g_hbm.at[0, 0, :, pl.ds(pl.multiple_of(b * 1280, 1280), 1280)], gs.at[i], load_sem.at[i]
        )
        for i, b in enumerate(blocks)
    ]
    consts = [
        pltpu.make_async_copy(src, dst, load_sem.at[4 + i])
        for i, (src, dst) in enumerate(
            [(c_right, right), (c_left, left), (m_hbm.at[0], ms), (c_pl, p_left), (c_pr, p_right)]
        )
    ]
    for copy in consts[:1] + loads + consts[1:]:
        copy.start()

    barrier = pltpu.get_barrier_semaphore()

    def signal(to, sem):
        pl.semaphore_signal(sem, inc=1, device_id=to, device_id_type=MESH)

    @pl.when(owner)
    def _():
        for dy in (4, 3, 5, 2, 6, 1, 7, 0):
            for dx in range(2):
                for dl in range(2):
                    if dx or dy or dl:
                        signal(device((xh + dx) % 2, z, (y + dy) % NY, (xl + dl) % 2, 0), barrier)
        for dz in (6, 5, 7, 4, 8, 3, 9, 2, 10, 1, 11):
            signal(device(xh, (z + dz) % NZ, y, xl, 1), barrier)

    @pl.when(jnp.logical_not(owner))
    def _():
        signal(device(xh, z, y, 1 - xl, 0), barrier)

    @pl.when(c == 1)
    def _():
        signal(sibling, barrier)

    consts[0].wait()
    ys = []
    for i in (2, 3):
        loads[i].wait()
        ys.append(columns_of(gs[i], right, True))
    consts[1].wait()
    zs = rows_of(jnp.concatenate(ys, 1), left[...])
    for i in (2, 3):
        q = chunks_of(zs[:, 384 * (i - 2) : 384 * (i - 1)])
        cf[i, 0:4], cf[i, 4:8], cf[i, 8:10] = q

    @pl.when(c == 0)
    def _():
        @pl.when(owner)
        def _():
            pl.semaphore_wait(barrier, 4 * NT - 1)

        @pl.when(jnp.logical_not(owner))
        def _():
            pl.semaphore_wait(barrier, 4 * NT + 3)

        signal(sibling, in_sem.at[0])

    @pl.when(c == 1)
    def _():
        pl.semaphore_wait(in_sem.at[0], 1)

    def send(src, dst, s, r, to):
        return pltpu.make_async_remote_copy(
            src_ref=src, dst_ref=dst, send_sem=s, recv_sem=r, device_id=to, device_id_type=MESH
        )

    core0 = send(cf.at[pl.ds(2, 2)], rc, core_s.at[0], core_r.at[0], sibling)
    core0.start()
    for t in range(NT):
        gst[0, t] = gs[3, :, 128 * t : 128 * t + 128].astype(F32)
    core1 = send(gst.at[0], rg.at[0], core_s.at[1], core_r.at[1], sibling)
    core1.start()
    ys = []
    for i in (0, 1):
        loads[i].wait()
        ys.append(columns_of(gs[i], right, True))
    consts[2].wait()
    m1, m2 = split(0.9 * ms[...])
    ys[0] = ys[0] + columns_of(m1, right, True) + columns_of(m2, right, False)
    zs = rows_of(jnp.concatenate(ys, 1), left[...])
    core0.wait_recv()
    for i in (0, 1):
        q = chunks_of(zs[:, 384 * i : 384 * (i + 1)])
        sa[i, 0:4] = q[0] + rc[i, 0:4]
        sa[i, 4:8] = q[1] + rc[i, 4:8]
        sa[i, 8:10] = q[2] + rc[i, 8:10]

    for i in range(2):
        for j, (ox, oy) in enumerate(ROWS_XY):
            to = device(ox, z, oy, xl if i == 0 else 1 - xl, c)
            copy = send(sa.at[i, j], ra.at[chip], a_sem.at[i], a_sem.at[2], to)
            if i == 0:
                here = jnp.logical_and(xh == ox, y == oy)

                @pl.when(jnp.logical_not(here))
                def _():
                    copy.start()

                @pl.when(here)
                def _():
                    ra[chip] = sa[0, j]
            else:
                copy.start()

    for t in range(NT):
        gst[1, t] = gs[2, :, 128 * t : 128 * t + 128].astype(F32)
    core2 = send(gst.at[1], rg.at[1], core_s.at[2], core_r.at[2], sibling)
    core2.start()
    core1.wait_recv()
    swaps = []
    for t in range(NT):
        xs[t] = gs[1, :, 128 * t : 128 * t + 128].astype(F32) + rg[0, t]
        swaps.append(send(xs.at[t], xt.at[t], x_s.at[t], x_r.at[t], across))
        swaps[-1].start()

    @pl.when(jnp.logical_and(owner, c == 1))
    def _():
        pl.semaphore_wait(barrier, 2 * (NZ - 1))
        signal(sibling, in_sem.at[1])

    @pl.when(owner)
    def _():
        send(ra.at[pl.ds(0, 31)], ra.at[pl.ds(0, 31)], a_sem.at[0], a_sem.at[2], sibling).wait_recv()
        total = ra[0]
        for i in range(1, 32):
            total = total + ra[i]
        sb[...] = total
        rb[z] = total

        @pl.when(c == 0)
        def _():
            pl.semaphore_wait(in_sem.at[1], 1)

        for dz in list(range(1, 7)) + list(range(11, 6, -1)):
            send(sb, rb.at[z], b_sem.at[0], b_sem.at[1], device(xh, (z + dz) % NZ, y, xl, c)).start()
        send(rb.at[pl.ds(0, 11)], rb.at[pl.ds(0, 11)], b_sem.at[0], b_sem.at[1], sibling).wait_recv()
        total = rb[0]
        for i in range(1, NZ):
            total = total + rb[i]
        sc[...] = total
        rt[mine] = total
        for dx in range(2):
            for dy in range(NY):
                if dx or dy:
                    to = device((xh + dx) % 2, z, (y + dy) % NY, xl, c)
                    send(sc, rt.at[mine], c_sem.at[0], c_sem.at[1], to).start()

    core2.wait_recv()
    consts[3].wait()
    consts[4].wait()
    outs = []
    for t in range(NT):
        cols = pl.ds(128 * t, 128)
        swaps[t].wait_recv()
        x = 0.9 * ms[:, cols] + ((gs[0, :, cols].astype(F32) + rg[1, t]) + xt[t])
        x1, x2 = split(x)
        u1, u2 = split(dot(p_left[...], jnp.concatenate([x1, x2, x1], 0)))
        om[:, cols] = x - dot(jnp.concatenate([u1, u2, u1], 1), p_right[...])
        outs.append(pltpu.make_async_copy(om.at[:, cols], new_m.at[0, :, cols], out_sem.at[t]))
        outs[-1].start()

    @pl.when(owner)
    def _():
        send(rt.at[pl.ds(0, 9)], rt.at[pl.ds(0, 9)], c_sem.at[0], c_sem.at[1], sibling).wait_recv()

    @pl.when(jnp.logical_not(owner))
    def _():
        send(rt, rt, c_sem.at[0], c_sem.at[1], sibling).wait_recv()

    outs.append(pltpu.make_async_copy(rt, totals, out_sem.at[NT]))
    outs[-1].start()

    for copy in (core0, core1, core2, *swaps):
        copy.wait_send()
    send(sa.at[1], sa.at[1], a_sem.at[1], a_sem.at[2], sibling).wait_send()

    @pl.when(owner)
    def _():
        send(sa.at[0, pl.ds(0, 9)], sa.at[0, pl.ds(0, 9)], a_sem.at[0], a_sem.at[2], sibling).wait_send()
        send(rb.at[pl.ds(0, 11)], rb.at[pl.ds(0, 11)], b_sem.at[0], b_sem.at[1], sibling).wait_send()
        send(ra.at[pl.ds(0, 15)], ra.at[pl.ds(0, 15)], c_sem.at[0], c_sem.at[1], sibling).wait_send()

    @pl.when(jnp.logical_not(owner))
    def _():
        send(sa.at[0], sa.at[0], a_sem.at[0], a_sem.at[2], sibling).wait_send()

    for copy in outs:
        copy.wait()


def finish(scale, totals, m_hbm, w_hbm, c_dl, c_dr, new_w, new_m, rt, vm, ws, d_left, d_right, ow, in_sem, out_sem):
    cuts = [pl.ds(0, 512), pl.ds(512, 512), pl.ds(1024, 256)]
    loads = [
        pltpu.make_async_copy(src, dst, in_sem.at[i])
        for i, (src, dst) in enumerate(
            [(totals, rt), (c_dl, d_left), (c_dr, d_right), (w_hbm, ws), *[(m_hbm.at[0, :, n], vm.at[:, n]) for n in cuts]]
        )
    ]
    for copy in loads:
        copy.start()
    for copy in loads[:4]:
        copy.wait()
    tail = rt[8:10].reshape(16, 128)
    zt = jnp.concatenate(
        [rt[0:4].reshape(32, 128), rt[4:8].reshape(32, 128), jnp.concatenate([tail, pltpu.roll(tail, 64, 1)], 0)], 1
    )
    z1, z2 = split(zt)
    v1, v2 = split(dot(d_left[...], jnp.concatenate([z1, z2, z1], 0)))
    outs = []
    for q, cols in enumerate(cuts):
        loads[4 + q].wait()
        outs.append(pltpu.make_async_copy(vm.at[:, cols], new_m.at[0, :, cols], out_sem.at[3 + q]))
        outs[-1].start()
        part = slice(128 * q, 128 * q + 128)
        low = dot(jnp.concatenate([v1[:, part], v2[:, part], v1[:, part]], 1), d_right[:, : cols.size])
        ow[:, cols] = ws[:, cols] - scale * low
        outs.append(pltpu.make_async_copy(ow.at[:, cols], new_w.at[:, cols], out_sem.at[q]))
        outs[-1].start()
    for copy in outs:
        copy.wait()


def solution(mesh):
    scale = float(1.0 / np.sqrt(np.float32(mesh.shape["rep"])))
    consts = constants()

    def per_device(gradient, momentum, params):
        vmem, dma = pltpu.VMEM, pltpu.SemaphoreType.DMA
        tiles = (NT, TILE, TILE)
        chunk = (8, 128)
        slab = (TILE, NT * TILE)

        def last(*refs):
            finish(scale, *refs)

        totals, new_m = pl.pallas_call(
            kernel,
            out_shape=(
                jax.ShapeDtypeStruct((NT, *chunk), F32),
                jax.ShapeDtypeStruct(momentum.shape, F32),
            ),
            in_specs=[pl.BlockSpec(memory_space=pl.ANY)] * 6,
            out_specs=(pl.BlockSpec(memory_space=pl.ANY),) * 2,
            scratch_shapes=[
                vmem((4, *slab), BF16), vmem(slab, F32),
                *[vmem(a.shape, BF16) for a in consts[:4]],
                vmem((4, NT, *chunk), F32),
                vmem((2, NT, *chunk), F32),
                vmem((2, NT, *chunk), F32),
                vmem((32, *chunk), F32),
                vmem(chunk, F32),
                vmem((NZ, *chunk), F32),
                vmem(chunk, F32),
                vmem((NT, *chunk), F32),
                vmem((2, *tiles), F32),
                vmem((2, *tiles), F32),
                vmem(tiles, F32),
                vmem(tiles, F32),
                vmem(slab, F32),
                dma((9,)), dma((3,)), dma((3,)), dma((3,)), dma((2,)), dma((2,)),
                dma((NT,)), dma((NT,)), dma((NT + 1,)), pltpu.SemaphoreType.REGULAR((2,)),
            ],
            compiler_params=pltpu.CompilerParams(
                collective_id=0, has_side_effects=True, vmem_limit_bytes=63 * 2**20
            ),
        )(gradient, momentum, *[jnp.asarray(a) for a in consts[:4]])
        return pl.pallas_call(
            last,
            out_shape=(
                jax.ShapeDtypeStruct(params.shape, F32),
                jax.ShapeDtypeStruct(momentum.shape, F32),
            ),
            in_specs=[pl.BlockSpec(memory_space=pl.ANY)] * 5,
            out_specs=(pl.BlockSpec(memory_space=pl.ANY),) * 2,
            scratch_shapes=[
                vmem((NT, *chunk), F32), vmem(slab, F32), vmem(slab, F32),
                *[vmem(a.shape, BF16) for a in consts[4:]], vmem(slab, F32), dma((7,)), dma((6,)),
            ],
            compiler_params=pltpu.CompilerParams(vmem_limit_bytes=63 * 2**20),
        )(totals, new_m, params, *[jnp.asarray(a) for a in consts[4:]])

    return jax.shard_map(
        per_device,
        mesh=mesh,
        in_specs=(P("rep", "fsdp", None, None), P("rep", None, "fsdp"), P(None, "fsdp")),
        out_specs=(P(None, "fsdp"), P("rep", None, "fsdp")),
        check_vma=False,
    )
```

```python
import jax
import jax.numpy as jnp
import numpy as np
from jax import lax
from jax.experimental import pallas as pl
from jax.experimental.pallas import tpu as pltpu
from jax.sharding import PartitionSpec as P

MESH = pl.DeviceIdType.MESH
F32, BF16 = jnp.float32, jnp.bfloat16
TILE, KEEP = 128, 32
NXH, NZ, NY = 2, 12, 8
FIRST, NC = 7, 5
ROWS_XY = [(0, (FIRST + j) % NY) for j in range(NC)]
FORWARD = {0: (11, 10, 9, 8), 1: (7,), 2: (3, 4, 5, 6)}
NT = 10


def split_np(a):
    a = np.asarray(a, np.float32)
    high = a.astype(jnp.bfloat16)
    low = (a - high.astype(np.float32)).astype(jnp.bfloat16)
    return high, low


def constants():
    k, n = np.arange(KEEP)[:, None], np.arange(TILE)[None, :]
    basis = np.cos(np.pi * (2 * n + 1) * k / (2 * TILE)) * np.sqrt(2 / TILE)
    basis = basis * np.where(k == 0, np.sqrt(0.5), 1.0)
    b1, b2 = split_np(basis)
    zero = np.zeros_like(b1)

    def four(b):
        out = np.zeros((4 * b.shape[0], 4 * b.shape[1]), b.dtype)
        for i in range(4):
            out[i * b.shape[0] : (i + 1) * b.shape[0], i * b.shape[1] : (i + 1) * b.shape[1]] = b
        return out

    right = np.concatenate([four(b1.T), four(b2.T)], 1)
    left = np.block([[b1, b1], [b2, zero]])
    p1, p2 = split_np(basis.T @ basis)
    p_left = np.concatenate([p1, p1, p2], 1)
    p_right = np.concatenate([p1, p1, p2], 0)
    d_left = np.concatenate([b1.T, b1.T, b2.T], 1)
    d_right = np.concatenate([four(b1), four(b1), four(b2)], 0)
    return right, left, p_left, p_right, d_left, d_right


def split(x):
    high = x.astype(BF16)
    return high, (x - high.astype(F32)).astype(BF16)


def dot(a, b):
    return jnp.dot(a, b, preferred_element_type=F32)


def columns_of(g, right, low):
    parts = []
    for q in range(3):
        width = 512 if q < 2 else 256
        x = g[:, 512 * q : 512 * q + width]
        if low:
            y = dot(x, right[:width, :])
            parts.append(y[:, :128] + y[:, 128:])
        else:
            parts.append(dot(x, right[:width, :128]))
    return jnp.concatenate(parts, 1)


def rows_of(y, left):
    y1, y2 = split(y)
    z = dot(left, jnp.concatenate([y1, y2], 0))
    return z[:KEEP] + z[KEEP:]


def chunks_of(z):
    tail = z[:, 256:384]
    tail = tail[:16] + pltpu.roll(tail[16:], 64, 1)
    return (
        z[:, :128].reshape(2, 16, 128),
        z[:, 128:256].reshape(2, 16, 128),
        tail.reshape(1, 16, 128),
    )


def kernel(
    g_hbm, m_hbm, c_right, c_left, c_pl, c_pr,
    totals, new_m,
    gs, ms, right, left, p_left, p_right,
    cf, rc, sa, ra, sb, rb, sc, rt,
    gst, rg, xs, xt, om,
    load_sem, core_s, core_r, a_sem, b_sem, c_sem, x_s, x_r, out_sem, in_sem, f_sem,
):
    rep, f = lax.axis_index("rep"), lax.axis_index("fsdp")
    xh, z, y = rep // (NZ * NY), (rep // NY) % NZ, rep % NY
    xl, c = f // 2, f % 2

    def device(dxh, dz, dy, dxl, dc):
        return ((dxh * NZ + dz) * NY + dy, dxl * 2 + dc)

    sibling = device(xh, z, y, xl, 1 - c)
    across = device(xh, z, y, 1 - xl, c)
    line = (y - FIRST + NY) % NY
    owner = jnp.logical_and(xh == 0, line < NC)
    mine = jnp.where(owner, line, 0)
    early = z < len(FORWARD)
    chip = (xh * NY + y) * 2 + xl

    blocks = [f, (1 - xl) * 2 + c, xl * 2 + 1 - c, (1 - xl) * 2 + 1 - c]
    loads = [
        pltpu.make_async_copy(
            g_hbm.at[0, 0, :, pl.ds(pl.multiple_of(b * 1280, 1280), 1280)], gs.at[i], load_sem.at[i]
        )
        for i, b in enumerate(blocks)
    ]
    consts = [
        pltpu.make_async_copy(src, dst, load_sem.at[4 + i])
        for i, (src, dst) in enumerate(
            [(c_right, right), (c_left, left), (m_hbm.at[0], ms), (c_pl, p_left), (c_pr, p_right)]
        )
    ]
    for copy in consts[:1] + loads[2:] + consts[1:2] + loads[:2] + consts[2:]:
        copy.start()

    barrier = pltpu.get_barrier_semaphore()

    def signal(to, sem):
        pl.semaphore_signal(sem, inc=1, device_id=to, device_id_type=MESH)

    @pl.when(owner)
    def _():
        for dy in (4, 3, 5, 2, 6, 1, 7, 0):
            for dx in range(2):
                for dl in range(2):
                    if dx or dy or dl:
                        signal(device((xh + dx) % 2, z, (y + dy) % NY, (xl + dl) % 2, 0), barrier)
        for dz in (6, 5, 7, 4, 8, 3, 9, 2, 10, 1, 11):
            signal(device(xh, (z + dz) % NZ, y, xl, 1), barrier)

    @pl.when(jnp.logical_not(owner))
    def _():
        signal(device(xh, z, y, 1 - xl, 0), barrier)

    @pl.when(c == 1)
    def _():
        signal(sibling, barrier)

    consts[0].wait()
    ys = []
    for i in (2, 3):
        loads[i].wait()
        ys.append(columns_of(gs[i], right, True))
    consts[1].wait()
    zs = rows_of(jnp.concatenate(ys, 1), left[...])
    for i in (2, 3):
        q = chunks_of(zs[:, 384 * (i - 2) : 384 * (i - 1)])
        cf[i, 0:2], cf[i, 2:4], cf[i, 4:5] = q

    @pl.when(c == 0)
    def _():
        @pl.when(owner)
        def _():
            pl.semaphore_wait(barrier, 4 * NC - 1)

        @pl.when(jnp.logical_not(owner))
        def _():
            pl.semaphore_wait(barrier, 4 * NC + 3)

        signal(sibling, in_sem.at[0])

    @pl.when(c == 1)
    def _():
        pl.semaphore_wait(in_sem.at[0], 1)

    def send(src, dst, s, r, to):
        return pltpu.make_async_remote_copy(
            src_ref=src, dst_ref=dst, send_sem=s, recv_sem=r, device_id=to, device_id_type=MESH
        )

    core0 = send(cf.at[pl.ds(2, 2)], rc, core_s.at[0], core_r.at[0], sibling)
    core0.start()
    for t in range(NT):
        gst[0, t] = gs[3, :, 128 * t : 128 * t + 128].astype(F32)
    core1 = send(gst.at[0], rg.at[0], core_s.at[1], core_r.at[1], sibling)
    core1.start()
    ys = []
    for i in (0, 1):
        loads[i].wait()
        ys.append(columns_of(gs[i], right, True))
    consts[2].wait()
    m1, m2 = split(0.9 * ms[...])
    ys[0] = ys[0] + columns_of(m1, right, True) + columns_of(m2, right, False)
    zs = rows_of(jnp.concatenate(ys, 1), left[...])
    core0.wait_recv()
    for i in (0, 1):
        q = chunks_of(zs[:, 384 * i : 384 * (i + 1)])
        sa[i, 0:2] = q[0] + rc[i, 0:2]
        sa[i, 2:4] = q[1] + rc[i, 2:4]
        sa[i, 4:5] = q[2] + rc[i, 4:5]

    for i in range(2):
        for j, (ox, oy) in enumerate(ROWS_XY):
            to = device(ox, z, oy, xl if i == 0 else 1 - xl, c)
            copy = send(sa.at[i, j], ra.at[chip], a_sem.at[i], a_sem.at[2], to)
            if i == 0:
                here = jnp.logical_and(xh == ox, y == oy)

                @pl.when(jnp.logical_not(here))
                def _():
                    copy.start()

                @pl.when(here)
                def _():
                    ra[chip] = sa[0, j]
            else:
                copy.start()

    for t in range(NT):
        gst[1, t] = gs[2, :, 128 * t : 128 * t + 128].astype(F32)
    core2 = send(gst.at[1], rg.at[1], core_s.at[2], core_r.at[2], sibling)
    core2.start()
    core1.wait_recv()
    swaps = []
    for t in range(NT):
        xs[t] = gs[1, :, 128 * t : 128 * t + 128].astype(F32) + rg[0, t]
        swaps.append(send(xs.at[t], xt.at[t], x_s.at[t], x_r.at[t], across))
        swaps[-1].start()

    @pl.when(jnp.logical_and(owner, c == 1))
    def _():
        pl.semaphore_wait(barrier, 2 * (NZ - 1))
        signal(sibling, in_sem.at[1])

    @pl.when(owner)
    def _():
        send(ra.at[pl.ds(0, 31)], ra.at[pl.ds(0, 31)], a_sem.at[0], a_sem.at[2], sibling).wait_recv()
        total = ra[0]
        for i in range(1, 32):
            total = total + ra[i]
        sb[...] = total
        rb[z] = total

        @pl.when(c == 0)
        def _():
            pl.semaphore_wait(in_sem.at[1], 1)

        for k in FORWARD:

            @pl.when(z != k)
            def _():
                send(sb, rb.at[z], b_sem.at[0], b_sem.at[1], device(xh, k, y, xl, c)).start()

        @pl.when(early)
        def _():
            send(rb.at[pl.ds(0, 11)], rb.at[pl.ds(0, 11)], b_sem.at[0], b_sem.at[1], sibling).wait_recv()
            total = rb[0]
            for i in range(1, NZ):
                total = total + rb[i]
            sc[...] = total

        @pl.when(jnp.logical_not(early))
        def _():
            send(sc, sc, f_sem.at[0], f_sem.at[1], sibling).wait_recv()

        rt[mine] = sc[...]
        for oy in (0, 1, 7, 2, 6, 3, 5, 4):
            for ox in range(NXH):

                @pl.when(jnp.logical_or(xh != ox, y != oy))
                def _():
                    send(sc, rt.at[mine], c_sem.at[0], c_sem.at[1], device(ox, z, oy, xl, c)).start()

        for k, others in FORWARD.items():

            @pl.when(z == k)
            def _():
                for other in others:
                    send(sc, sc, f_sem.at[0], f_sem.at[1], device(xh, other, y, xl, c)).start()

    core2.wait_recv()
    consts[3].wait()
    consts[4].wait()
    outs = []
    for t in range(NT):
        cols = pl.ds(128 * t, 128)
        swaps[t].wait_recv()
        x = 0.9 * ms[:, cols] + ((gs[0, :, cols].astype(F32) + rg[1, t]) + xt[t])
        x1, x2 = split(x)
        u1, u2 = split(dot(p_left[...], jnp.concatenate([x1, x2, x1], 0)))
        om[:, cols] = x - dot(jnp.concatenate([u1, u2, u1], 1), p_right[...])
        outs.append(pltpu.make_async_copy(om.at[:, cols], new_m.at[0, :, cols], out_sem.at[t]))
        outs[-1].start()

    @pl.when(owner)
    def _():
        send(rt.at[pl.ds(0, NC - 1)], rt.at[pl.ds(0, NC - 1)], c_sem.at[0], c_sem.at[1], sibling).wait_recv()

    @pl.when(jnp.logical_not(owner))
    def _():
        send(rt, rt, c_sem.at[0], c_sem.at[1], sibling).wait_recv()

    outs.append(pltpu.make_async_copy(rt, totals, out_sem.at[NT]))
    outs[-1].start()

    for copy in (core0, core1, core2, *swaps):
        copy.wait_send()
    send(sa.at[1], sa.at[1], a_sem.at[1], a_sem.at[2], sibling).wait_send()

    @pl.when(owner)
    def _():
        send(sa.at[0, pl.ds(0, NC - 1)], sa.at[0, pl.ds(0, NC - 1)], a_sem.at[0], a_sem.at[2], sibling).wait_send()
        few = pl.ds(0, len(FORWARD) - 1)
        send(rb.at[few], rb.at[few], b_sem.at[0], b_sem.at[1], sibling).wait_send()

        @pl.when(jnp.logical_not(early))
        def _():
            send(sb, sb, b_sem.at[0], b_sem.at[1], sibling).wait_send()

        for k, others in FORWARD.items():

            @pl.when(z == k)
            def _():
                all_of = pl.ds(0, len(others))
                send(rb.at[all_of], rb.at[all_of], f_sem.at[0], f_sem.at[1], sibling).wait_send()

        send(ra.at[pl.ds(0, 15)], ra.at[pl.ds(0, 15)], c_sem.at[0], c_sem.at[1], sibling).wait_send()

    @pl.when(jnp.logical_not(owner))
    def _():
        send(sa.at[0], sa.at[0], a_sem.at[0], a_sem.at[2], sibling).wait_send()

    for copy in outs:
        copy.wait()


def finish(scale, totals, m_hbm, w_hbm, c_dl, c_dr, new_w, new_m, rt, vm, ws, d_left, d_right, ow, in_sem, out_sem):
    cuts = [pl.ds(0, 512), pl.ds(512, 512), pl.ds(1024, 256)]
    loads = [
        pltpu.make_async_copy(src, dst, in_sem.at[i])
        for i, (src, dst) in enumerate(
            [(totals, rt), (c_dl, d_left), (c_dr, d_right), (w_hbm, ws), *[(m_hbm.at[0, :, n], vm.at[:, n]) for n in cuts]]
        )
    ]
    for copy in loads:
        copy.start()
    for copy in loads[:4]:
        copy.wait()
    tail = rt[4]
    zt = jnp.concatenate(
        [rt[0:2].reshape(32, 128), rt[2:4].reshape(32, 128), jnp.concatenate([tail, pltpu.roll(tail, 64, 1)], 0)], 1
    )
    z1, z2 = split(zt)
    v1, v2 = split(dot(d_left[...], jnp.concatenate([z1, z2, z1], 0)))
    outs = []
    for q, cols in enumerate(cuts):
        loads[4 + q].wait()
        outs.append(pltpu.make_async_copy(vm.at[:, cols], new_m.at[0, :, cols], out_sem.at[3 + q]))
        outs[-1].start()
        part = slice(128 * q, 128 * q + 128)
        low = dot(jnp.concatenate([v1[:, part], v2[:, part], v1[:, part]], 1), d_right[:, : cols.size])
        ow[:, cols] = ws[:, cols] - scale * low
        outs.append(pltpu.make_async_copy(ow.at[:, cols], new_w.at[:, cols], out_sem.at[q]))
        outs[-1].start()
    for copy in outs:
        copy.wait()


def solution(mesh):
    scale = float(1.0 / np.sqrt(np.float32(mesh.shape["rep"])))
    consts = constants()

    def per_device(gradient, momentum, params):
        vmem, dma = pltpu.VMEM, pltpu.SemaphoreType.DMA
        tiles = (NT, TILE, TILE)
        chunk = (16, 128)
        slab = (TILE, NT * TILE)

        def last(*refs):
            finish(scale, *refs)

        totals, new_m = pl.pallas_call(
            kernel,
            out_shape=(
                jax.ShapeDtypeStruct((NC, *chunk), F32),
                jax.ShapeDtypeStruct(momentum.shape, F32),
            ),
            in_specs=[pl.BlockSpec(memory_space=pl.ANY)] * 6,
            out_specs=(pl.BlockSpec(memory_space=pl.ANY),) * 2,
            scratch_shapes=[
                vmem((4, *slab), BF16), vmem(slab, F32),
                *[vmem(a.shape, BF16) for a in consts[:4]],
                vmem((4, NC, *chunk), F32),
                vmem((2, NC, *chunk), F32),
                vmem((2, NC, *chunk), F32),
                vmem((32, *chunk), F32),
                vmem(chunk, F32),
                vmem((NZ, *chunk), F32),
                vmem(chunk, F32),
                vmem((NC, *chunk), F32),
                vmem((2, *tiles), F32),
                vmem((2, *tiles), F32),
                vmem(tiles, F32),
                vmem(tiles, F32),
                vmem(slab, F32),
                dma((9,)), dma((3,)), dma((3,)), dma((3,)), dma((2,)), dma((2,)),
                dma((NT,)), dma((NT,)), dma((NT + 1,)), pltpu.SemaphoreType.REGULAR((2,)), dma((2,)),
            ],
            compiler_params=pltpu.CompilerParams(
                collective_id=0, has_side_effects=True, vmem_limit_bytes=63 * 2**20
            ),
        )(gradient, momentum, *[jnp.asarray(a) for a in consts[:4]])
        return pl.pallas_call(
            last,
            out_shape=(
                jax.ShapeDtypeStruct(params.shape, F32),
                jax.ShapeDtypeStruct(momentum.shape, F32),
            ),
            in_specs=[pl.BlockSpec(memory_space=pl.ANY)] * 5,
            out_specs=(pl.BlockSpec(memory_space=pl.ANY),) * 2,
            scratch_shapes=[
                vmem((NC, *chunk), F32), vmem(slab, F32), vmem(slab, F32),
                *[vmem(a.shape, BF16) for a in consts[4:]], vmem(slab, F32), dma((7,)), dma((6,)),
            ],
            compiler_params=pltpu.CompilerParams(vmem_limit_bytes=63 * 2**20),
        )(totals, new_m, params, *[jnp.asarray(a) for a in consts[4:]])

    return jax.shard_map(
        per_device,
        mesh=mesh,
        in_specs=(P("rep", "fsdp", None, None), P("rep", None, "fsdp"), P(None, "fsdp")),
        out_specs=(P(None, "fsdp"), P("rep", None, "fsdp")),
        check_vma=False,
    )
```
